128 devices in a mesh: row: 16 (over x, z_hi, core), col: 8 (over y, z_lo).
Axes of the slice: x: 4, y: 4, z: 4 (z_hi: 2, z_lo: 2; z = z_hi * 2 + z_lo), core: 2. Of those that a mesh axis runs over, the one named last changes fastest.
Arguments:
- loads: float32 [3, 24576], P(None, 'row'), may hold values from -6 to 6
- nd_source: int32 [24576], P('row'), may hold values from 0 to 24575, as said below
- panel: bfloat16 [24576, 512], P('row', 'col'), as said below
- trailing: bfloat16 [24576, 24576], P('row', 'col'), may hold values from -6 to 6
- pattern: int32 [192, 192], P('row', 'col'), may hold values from 0 to 1
- owner: int32 [16], replicated, may hold values from 0 to 15, each once
Outputs:
- loads_out: float32 [3, 24576], P(None, 'row')
- trailing_out: bfloat16 [24576, 24576], P('row', 'col')
The draws below stay inside these ranges and needn't reach their ends.
Inputs may be any that keep to these rules, and one draw needn't show every extreme that they name: `nd_source`: a permutation; the rows t * 1536 to (t + 1) * 1536 - 1 take, from each block s of 1536 columns, exactly the columns s * 1536 + t * 96 to s * 1536 + (t + 1) * 96 - 1. `panel`: the 512 x 512 block at rows owner[0] * 1536 has a positive definite symmetric part. `owner`: a permutation of the row indices.
All inputs are finite; a program needn't handle non-finite values.
Results may differ from the reference program's by a relative error of at most 0.005.
Values may be sent and summed in bfloat16 or wider, within the bound.
No kernel may reach another device: no remote copies, remote signals or barrier semaphores. Data moves between devices by JAX's collectives and lax.ppermute only.
A program may use at most 128 MiB of HBM per device.

```python
import math
import jax
import jax.numpy as jnp
from jax import lax

M = 24576
PIV = 512
BLK = 128
RD = 1536
Q = 96
N_ROW = 16


def draw_nd_source(key, part):
    target = jnp.arange(N_ROW, dtype=jnp.int32)[:, None]
    column = jnp.arange(RD, dtype=jnp.int32)[None, :]
    source_base = column // Q * RD + target * Q + column % Q
    key_list = jax.random.split(key, N_ROW)
    shuffle = jax.vmap(lambda subkey: jax.random.permutation(subkey, RD))(key_list)
    return jnp.take_along_axis(source_base, shuffle, axis=1).reshape(M).astype(jnp.int32)


def draw_panel(key, part):
    key_first, key_second = jax.random.split(jax.random.fold_in(key, 11))
    rows = jnp.arange(M, dtype=jnp.int32)[:, None]
    cols = jnp.arange(PIV, dtype=jnp.int32)[None, :]
    offset = rows % RD
    general = 0.3 * jax.random.normal(key_first, (M, PIV), jnp.float32)
    small = jax.random.uniform(key_second, (M, PIV), jnp.float32, -1.0, 1.0) * (1.5 / math.sqrt(PIV))
    diagonal = jnp.where(offset == cols, 3.0, 0.0)
    return jnp.where(offset < PIV, small + diagonal, general).astype(jnp.bfloat16)


def draw_pattern(key, part):
    key_first, key_second = jax.random.split(jax.random.fold_in(key, 23))
    count = M // BLK
    active = jax.random.randint(key_first, (count, 1), 0, 3) == 0
    filled = jax.random.randint(key_second, (count, count), 0, 2) == 1
    return (active & filled).astype(jnp.int32)


def levels(own_key, extent, cuts, smallest, high):
    def one(dim, blocks):
        steps = jax.random.uniform(jax.random.fold_in(jax.random.fold_in(own_key, 6), dim), (blocks,), jnp.float32, smallest / len(cuts), high / len(cuts))
        return jnp.repeat(jnp.exp(steps), extent[dim] // blocks).reshape((-1,) + (1,) * (len(extent) - dim - 1))

    loudness = one(*cuts[0])
    for cut in cuts[1:]:
        loudness = loudness * one(*cut)
    return loudness


def gaussian(rng, shape, spread, most, cuts=(), kind=jnp.bfloat16):
    values = jax.random.normal(rng, shape, jnp.float32) * spread
    if len(cuts) > 0:
        values = levels(rng, shape, cuts, -0.22, 0.18) * values
    return jnp.clip(values, min=-most, max=most).astype(kind)


def setup_inputs(seed: int = 0) -> dict:
    keys = jax.random.split(jax.random.key(seed), 7)
    return {
        "loads": gaussian(keys[0], (3, M), 1.0, 6.0, ((1, 16),), jnp.float32),
        "nd_source": draw_nd_source(jax.random.fold_in(keys[6], 71), 0),
        "panel": draw_panel(jax.random.fold_in(keys[6], 71), 0),
        "trailing": gaussian(keys[3], (M, M), 1.0, 6.0, ((0, 16), (1, 8))),
        "pattern": draw_pattern(jax.random.fold_in(keys[6], 71), 0),
        "owner": jax.random.permutation(keys[5], N_ROW).astype(jnp.int32),
    }


def reference(loads, nd_source, panel, trailing, pattern, owner):
    regrouped = jnp.take(loads, nd_source, axis=1)
    pivot_start = owner[0].astype(jnp.int32) * RD
    pivot_block = lax.dynamic_slice_in_dim(panel, pivot_start, PIV, 0).astype(jnp.float32)
    symmetric = 0.5 * (pivot_block + pivot_block.T)
    lower_factor = jnp.linalg.cholesky(symmetric)
    inverse = lax.linalg.triangular_solve(lower_factor, jnp.eye(PIV, dtype=jnp.float32), left_side=True, lower=True)
    inverse_half = inverse.astype(jnp.bfloat16)
    factor = jnp.dot(panel.astype(jnp.float32), inverse_half.T.astype(jnp.float32), preferred_element_type=jnp.float32).astype(jnp.bfloat16)
    pivot_loads = lax.dynamic_slice_in_dim(regrouped, pivot_start, PIV, 1)
    pivot_solve = jnp.dot(inverse, pivot_loads.T, precision=lax.Precision.HIGHEST)
    update = jnp.dot(factor.astype(jnp.float32), pivot_solve, precision=lax.Precision.HIGHEST).T
    positions = jnp.arange(M, dtype=jnp.int32)
    in_pivot = (positions >= pivot_start) & (positions < pivot_start + PIV)
    pivot_offset = jnp.clip(positions - pivot_start, 0, PIV - 1)
    loads_out = jnp.where(in_pivot[None, :], jnp.take(pivot_solve.T, pivot_offset, axis=1), regrouped - update)
    block_rows = RD // BLK
    block_cols = M // BLK

    def row_update(index):
        row_block = lax.dynamic_slice_in_dim(factor, index * RD, RD, 0)
        product = jnp.dot(row_block.astype(jnp.float32), factor.T.astype(jnp.float32), preferred_element_type=jnp.float32)
        old_rows = lax.dynamic_slice_in_dim(trailing, index * RD, RD, 0).astype(jnp.float32)
        flags = lax.dynamic_slice_in_dim(pattern, index * block_rows, block_rows, 0).astype(jnp.float32)
        masked = (product.reshape(block_rows, BLK, block_cols, BLK) * flags[:, None, :, None]).reshape(RD, M)
        return (old_rows - masked).astype(jnp.bfloat16)
    trailing_out = lax.map(row_update, jnp.arange(N_ROW, dtype=jnp.int32)).reshape(M, M)
    return (loads_out, trailing_out)
```

```python
import jax
import jax.numpy as jnp
from jax import lax
from jax.experimental import pallas as pl
from jax.experimental.pallas import tpu as pltpu
from jax.sharding import PartitionSpec as P

HI = lax.Precision.HIGHEST
F32 = jnp.float32
BF16 = jnp.bfloat16
BLOCK = 128

X_SHIFT = {k: [(i, (i // 4 + k) % 4 * 4 + i % 4) for i in range(16)] for k in (1, 2, 3)}
Y_SHIFT = {k: [(i, (i // 2 + k) % 4 * 2 + i % 2) for i in range(8)] for k in (1, 2, 3)}
Z_HI = [(i, i ^ 2) for i in range(16)]
CORE = [(i, i ^ 1) for i in range(16)]
Z_LO = [(i, i ^ 1) for i in range(8)]


def transposed_place():
    pairs = []
    for row in range(16):
        for col in range(8):
            x, z_hi, core = row // 4, row // 2 % 2, row % 2
            y, z_lo = col // 2, col % 2
            pairs.append((row * 8 + col, ((y * 2 + z_lo) * 2 + core) * 8 + x * 2 + z_hi))
    return pairs


def pair_up(mine, bit, perm, axis):
    other = lax.ppermute(mine, axis, perm)
    low = jnp.where(bit == 0, mine, other)
    high = jnp.where(bit == 0, other, mine)
    return jnp.concatenate([low, high], 0)


def ring(mine, shifts, axis):
    return [mine] + [lax.ppermute(mine, axis, shifts[k]) for k in (1, 2, 3)]


def select_root(mine, row_place, root):
    x, root_x = row_place // 4, root // 4
    pieces = ring(mine, X_SHIFT, "row")
    back = (x - root_x) % 4
    mine = jnp.where(
        back == 0, pieces[0], jnp.where(back == 1, pieces[1], jnp.where(back == 2, pieces[2], pieces[3]))
    )
    other = lax.ppermute(mine, "row", Z_HI)
    mine = jnp.where(row_place // 2 % 2 == root // 2 % 2, mine, other)
    other = lax.ppermute(mine, "row", CORE)
    return jnp.where(row_place % 2 == root % 2, mine, other)


def block_inverse(rows):
    n = rows[0].shape[1]
    lane = lax.broadcasted_iota(jnp.int32, (8, n), 1)
    sub = lax.broadcasted_iota(jnp.int32, (8, n), 0)
    rows = list(rows)
    out = []
    for g in range(len(rows)):
        p = 8 * g
        below = range(g + 1, len(rows))
        strip = rows[g]
        cols = [jnp.broadcast_to(strip[:, p + k : p + k + 1], (8, n)) for k in range(8)]
        cols_below = {
            i: [jnp.broadcast_to(rows[i][:, p + k : p + k + 1], (8, n)) for k in range(8)] for i in below
        }
        in_block = (lane >= p) & (lane < p + 8)
        for i in below:
            rows[i] = jnp.where(in_block, 0.0, rows[i])
        pivots = None
        for k in range(8):
            d = jnp.broadcast_to(cols[k][k : k + 1, :], (8, n))
            r = 1.0 / d
            pivots = d if k == 0 else jnp.where(sub == k, d, pivots)
            m = jnp.where(sub > k, cols[k] * r, 0.0)
            piv = jnp.where(lane == p + k, 1.0, jnp.broadcast_to(strip[k : k + 1, :], (8, n)))
            strip = jnp.where((lane == p + k) & (sub > k), 0.0, strip) - m * piv
            piv = jnp.where((lane > p + k) & (lane < p + 8), 0.0, piv)
            u = [None] * 8
            for q in range(k + 1, 8):
                u[q] = jnp.broadcast_to(cols[q][k : k + 1, :], (8, n))
                cols[q] = cols[q] - m * u[q]
            for i in below:
                f = cols_below[i][k] * r
                for q in range(k + 1, 8):
                    cols_below[i][q] = cols_below[i][q] - f * u[q]
                rows[i] = rows[i] - f * piv
        s = lax.rsqrt(pivots)
        out.append(jnp.where(lane == sub + p, s, strip * s))
    return out


def inverse_kernel(place_ref, p0, p1, p2, p3, w_ref, half_ref, g_ref):
    n = w_ref.shape[0]
    B = BLOCK
    for k, piece in enumerate((p0, p1, p2, p3)):
        at = pl.multiple_of((place_ref[0] + 4 - k) % 4 * B, B)
        g_ref[pl.ds(at, B), :] = piece[...].astype(F32)
    whole = g_ref[...]
    g_ref[...] = 0.5 * (whole + whole.T)
    lane = lax.broadcasted_iota(jnp.int32, (B, n), 1)
    row = lax.broadcasted_iota(jnp.int32, (B, n), 0)
    lane_b = lax.broadcasted_iota(jnp.int32, (B, B), 1)
    row_b = lax.broadcasted_iota(jnp.int32, (B, B), 0)

    def step(k, carry):
        at = pl.multiple_of(k * B, B)
        diag = g_ref[pl.ds(at, B), pl.ds(at, B)]
        wk = jnp.concatenate(block_inverse([diag[8 * i : 8 * i + 8] for i in range(B // 8)]), 0)
        wk = jnp.where(lane_b <= row_b, wk, 0.0)
        here = (lane >= at) & (lane < at + B)
        strip = jnp.where(here, jnp.where(lane == row + at, 1.0, 0.0), g_ref[pl.ds(at, B), :])
        y = jnp.dot(wk, strip, precision=HI, preferred_element_type=F32)
        done = jnp.where(lane <= row + at, y, 0.0)
        w_ref[pl.ds(at, B), :] = done
        half_ref[pl.ds(at, B), :] = done.astype(BF16)
        for j in range(1, n // B):

            @pl.when(j > k)
            def _():
                old = jnp.where(here, 0.0, g_ref[j * B : (j + 1) * B, :])
                g_ref[j * B : (j + 1) * B, :] = old - lax.dot_general(
                    y[:, j * B : (j + 1) * B],
                    y,
                    (((0,), (0,)), ((), ())),
                    precision=HI,
                    preferred_element_type=F32,
                )

        return carry

    lax.fori_loop(0, n // B, step, 0)


def inverse_of(pieces, y):
    n = pieces[0].shape[1]
    vmem = pl.BlockSpec(memory_space=pltpu.VMEM)
    return pl.pallas_call(
        inverse_kernel,
        out_shape=(jax.ShapeDtypeStruct((n, n), F32), jax.ShapeDtypeStruct((n, n), BF16)),
        in_specs=[pl.BlockSpec(memory_space=pltpu.SMEM)] + [vmem] * 4,
        out_specs=(vmem, vmem),
        scratch_shapes=[pltpu.VMEM((n, n), F32)],
        compiler_params=pltpu.CompilerParams(vmem_limit_bytes=24 << 20),
        cost_estimate=pl.CostEstimate(flops=2 * n**3, bytes_accessed=4 * n * n, transcendentals=0),
    )(y.reshape(1), *pieces)


def update_kernel(place_ref, pattern_ref, *refs):
    rows_in, first_in, second_in = refs[0:4], refs[4:8], refs[8:12]
    w_ref, half_ref, loads_ref, pivot_ref, trailing_ref, out_ref, loads_out_ref = refs[12:19]
    raw_ref, factor_ref, other_ref = refs[19:22]
    n = half_ref.shape[0]
    row_dev = rows_in[0].shape[1]
    tile = out_ref.shape[1]
    step = pl.program_id(0)
    x, y, core, is_owner = place_ref[0], place_ref[1], place_ref[2], place_ref[3]

    def factor_of(pieces, spot, target, column):
        for k, piece in enumerate(pieces):
            at = pl.multiple_of((spot + 4 - k) % 4 * BLOCK, BLOCK)
            raw_ref[pl.ds(at, BLOCK), :] = piece[...]
        for c in range(0, row_dev, 512):
            part = jnp.dot(half_ref[...], raw_ref[:, c : c + 512], preferred_element_type=F32).astype(BF16)
            target[:, pl.ds(pl.multiple_of(column + c, 128), 512)] = part

    @pl.when(step == 0)
    def _():
        factor_of(first_in, x, other_ref, core * row_dev)
        factor_of(second_in, x, other_ref, (1 - core) * row_dev)
        for k, piece in enumerate(rows_in):
            at = pl.multiple_of((y + 4 - k) % 4 * BLOCK, BLOCK)
            raw_ref[pl.ds(at, BLOCK), :] = piece[...]
        for c in range(0, row_dev, 512):
            part = lax.dot_general(
                raw_ref[:, c : c + 512], half_ref[...], (((0,), (1,)), ((), ())), preferred_element_type=F32
            )
            factor_ref[c : c + 512, :] = part.astype(BF16)
        solve = lax.dot_general(
            pivot_ref[...], w_ref[...], (((1,), (1,)), ((), ())), precision=HI, preferred_element_type=F32
        )
        change = lax.dot_general(
            solve, factor_ref[...].astype(F32), (((1,), (1,)), ((), ())), precision=HI, preferred_element_type=F32
        )
        loads_out_ref[...] = loads_ref[...] - change

        @pl.when(is_owner == 1)
        def _():
            loads_out_ref[:, :n] = solve

    columns = other_ref[:, pl.ds(pl.multiple_of(step * tile, tile), tile)]
    for b in range(0, row_dev, 512):
        product = jnp.dot(factor_ref[b : b + 512, :], columns, preferred_element_type=F32)
        for i in range(0, 512, BLOCK):
            for j in range(0, tile, BLOCK):
                flag = pattern_ref[(b + i) // BLOCK, step * (tile // BLOCK) + j // BLOCK].astype(F32)
                old = trailing_ref[b + i : b + i + BLOCK, j : j + BLOCK].astype(F32)
                new = old - product[i : i + BLOCK, j : j + BLOCK] * flag
                out_ref[b + i : b + i + BLOCK, j : j + BLOCK] = new.astype(BF16)


def update(place, pattern, rows, first, second, w, half, regrouped, pivot_loads, trailing):
    row_dev, col_dev = trailing.shape
    n = half.shape[0]
    tile = 256
    smem = pl.BlockSpec(memory_space=pltpu.SMEM)
    vmem = pl.BlockSpec(memory_space=pltpu.VMEM)
    tiled = pl.BlockSpec((row_dev, tile), lambda s: (0, s))
    return pl.pallas_call(
        update_kernel,
        grid=(col_dev // tile,),
        out_shape=(
            jax.ShapeDtypeStruct((row_dev, col_dev), BF16),
            jax.ShapeDtypeStruct((8, row_dev), F32),
        ),
        in_specs=[smem, smem] + [vmem] * 16 + [tiled],
        out_specs=(tiled, vmem),
        scratch_shapes=[
            pltpu.VMEM((n, row_dev), BF16),
            pltpu.VMEM((row_dev, n), BF16),
            pltpu.VMEM((n, col_dev), BF16),
        ],
        compiler_params=pltpu.CompilerParams(vmem_limit_bytes=48 << 20),
        cost_estimate=pl.CostEstimate(flops=8 << 30, bytes_accessed=24 << 20, transcendentals=0),
    )(place, pattern, *rows, *first, *second, w, half, regrouped, pivot_loads, trailing)


def per_device(loads, nd_source, panel, trailing, pattern, owner):
    row_dev = panel.shape[0]
    row_count = lax.axis_size("row")
    pivot_size = panel.shape[1] * lax.axis_size("col")
    share_size = row_dev // row_count
    row_place = lax.axis_index("row")
    col_place = lax.axis_index("col")
    root = owner[0]
    x, z_hi, core = row_place // 4, row_place // 2 % 2, row_place % 2
    y, z_lo = col_place // 2, col_place % 2
    mine = panel.T

    pivot = select_root(mine[:, :pivot_size], row_place, root)
    pivot = ring(pair_up(pivot, z_lo, Z_LO, "col"), Y_SHIFT, "col")
    w, half = inverse_of(pivot, y)

    arrived = lax.all_to_all(loads, "row", split_axis=1, concat_axis=1, tiled=True)
    slot = nd_source // row_dev * share_size + (nd_source % row_dev - row_place * share_size)
    regrouped = jnp.take(arrived, slot, axis=1)
    regrouped = jnp.pad(regrouped, ((0, 5), (0, 0)))
    pivot_loads = select_root(regrouped[:, :pivot_size], row_place, root)

    rows = ring(pair_up(mine, z_lo, Z_LO, "col"), Y_SHIFT, "col")
    moved = lax.ppermute(mine, ("row", "col"), transposed_place())
    first = ring(pair_up(moved, z_hi, Z_HI, "row"), X_SHIFT, "row")
    second = [lax.ppermute(piece, "row", CORE) for piece in first]

    place = jnp.stack([x, y, core, (row_place == root).astype(jnp.int32)]).astype(jnp.int32)
    trailing_out, loads_out = update(
        place, pattern, rows, first, second, w, half, regrouped, pivot_loads, trailing
    )
    return loads_out[:3], trailing_out


def solution(mesh):
    return jax.shard_map(
        per_device,
        mesh=mesh,
        in_specs=(P(None, "row"), P("row"), P("row", "col"), P("row", "col"), P("row", "col"), P()),
        out_specs=(P(None, "row"), P("row", "col")),
        check_vma=False,
    )
```

```python
import jax
import jax.numpy as jnp
from jax import lax
from jax.experimental import pallas as pl
from jax.experimental.pallas import tpu as pltpu
from jax.sharding import PartitionSpec as P

HI = lax.Precision.HIGHEST
F32 = jnp.float32
BF16 = jnp.bfloat16
BLOCK = 128

X_SHIFT = {k: [(i, (i // 4 + k) % 4 * 4 + i % 4) for i in range(16)] for k in (1, 2, 3)}
Y_SHIFT = {k: [(i, (i // 2 + k) % 4 * 2 + i % 2) for i in range(8)] for k in (1, 2, 3)}
Z_HI = [(i, i ^ 2) for i in range(16)]
CORE = [(i, i ^ 1) for i in range(16)]
Z_LO = [(i, i ^ 1) for i in range(8)]


def transposed_place():
    pairs = []
    for row in range(16):
        for col in range(8):
            x, z_hi, core = row // 4, row // 2 % 2, row % 2
            y, z_lo = col // 2, col % 2
            pairs.append((row * 8 + col, ((y * 2 + z_lo) * 2 + core) * 8 + x * 2 + z_hi))
    return pairs


def pair_up(mine, bit, perm, axis):
    other = lax.ppermute(mine, axis, perm)
    low = jnp.where(bit == 0, mine, other)
    high = jnp.where(bit == 0, other, mine)
    return jnp.concatenate([low, high], 0)


def ring(mine, shifts, axis):
    return [mine] + [lax.ppermute(mine, axis, shifts[k]) for k in (1, 2, 3)]


def after(value, *others):
    return lax.optimization_barrier((value, others))[0]


def pack_kernel(panel_ref, loads_ref, source_ref, out_ref):
    size = out_ref.shape[1] // 3
    source = source_ref[:, :size]
    digits = jnp.concatenate([source // BLOCK, source % BLOCK, jnp.zeros((6, size), jnp.int32)], 0)
    head = jnp.concatenate([panel_ref[:, :size].astype(F32), digits.astype(F32)], 0)
    loads = loads_ref[...]
    high = loads.astype(BF16).astype(F32)
    low = loads - high
    tail = jnp.concatenate([high, low, jnp.zeros((2, loads.shape[1]), F32)], 0)
    for c in range(3):
        out_ref[:24, c * size : (c + 1) * size] = head[24 * c : 24 * c + 24].astype(BF16)
    out_ref[24:, :] = tail.astype(BF16)


def pack(mine, loads, source):
    return pl.pallas_call(
        pack_kernel, out_shape=jax.ShapeDtypeStruct((32, mine.shape[1]), BF16)
    )(mine, loads, source[None])


def spread(packet, row_place, root):
    back = (row_place // 4 - root // 4) % 4
    pieces = ring(packet, X_SHIFT, "row")
    head = pieces[3][:24]
    for k in (2, 1, 0):
        head = jnp.where(back == k, pieces[k][:24], head)
    packet = jnp.concatenate([head] + [piece[24:] for piece in pieces], 0)
    for bit, perm in ((2, Z_HI), (1, CORE)):
        other = lax.ppermute(packet, "row", perm)
        head = jnp.where((row_place & bit) == (root & bit), packet[:24], other[:24])
        packet = jnp.concatenate([head, packet[24:], other[24:]], 0)
    return packet


def regroup(window_of, source, row_place, target, share):
    arrived = lax.dynamic_slice_in_dim(window_of, target * share, share, 2)
    arrived = arrived.transpose(1, 0, 2).reshape(arrived.shape[1], -1)
    home = source // (share * 16)
    flip = home ^ row_place
    turn = (row_place // 4 - home // 4) % 4
    place = ((flip & 1) * 2 + (flip // 2 & 1)) * 4 + turn
    slot = place * share + source % (share * 16) - target * share
    parts = jnp.take(arrived, slot, axis=1)
    return jnp.concatenate([parts[:3].astype(F32) + parts[3:6].astype(F32), jnp.zeros((5, slot.shape[0]), F32)], 0)


def block_inverse(rows):
    n = rows[0].shape[1]
    lane = lax.broadcasted_iota(jnp.int32, (8, n), 1)
    sub = lax.broadcasted_iota(jnp.int32, (8, n), 0)
    rows = list(rows)
    out = []
    for g in range(len(rows)):
        p = 8 * g
        below = range(g + 1, len(rows))
        strip = rows[g]
        cols = [jnp.broadcast_to(strip[:, p + k : p + k + 1], (8, n)) for k in range(8)]
        cols_below = {
            i: [jnp.broadcast_to(rows[i][:, p + k : p + k + 1], (8, n)) for k in range(8)] for i in below
        }
        in_block = (lane >= p) & (lane < p + 8)
        for i in below:
            rows[i] = jnp.where(in_block, 0.0, rows[i])
        pivots = None
        for k in range(8):
            d = jnp.broadcast_to(cols[k][k : k + 1, :], (8, n))
            r = 1.0 / d
            pivots = d if k == 0 else jnp.where(sub == k, d, pivots)
            m = jnp.where(sub > k, cols[k] * r, 0.0)
            piv = jnp.where(lane == p + k, 1.0, jnp.broadcast_to(strip[k : k + 1, :], (8, n)))
            strip = jnp.where((lane == p + k) & (sub > k), 0.0, strip) - m * piv
            piv = jnp.where((lane > p + k) & (lane < p + 8), 0.0, piv)
            u = [None] * 8
            for q in range(k + 1, 8):
                u[q] = jnp.broadcast_to(cols[q][k : k + 1, :], (8, n))
                cols[q] = cols[q] - m * u[q]
            for i in below:
                f = cols_below[i][k] * r
                for q in range(k + 1, 8):
                    cols_below[i][q] = cols_below[i][q] - f * u[q]
                rows[i] = rows[i] - f * piv
        s = lax.rsqrt(pivots)
        out.append(jnp.where(lane == sub + p, s, strip * s))
    return out


def eliminate(g_ref, w_ref, half_ref, blocks, first_row):
    n = g_ref.shape[0]
    B = BLOCK
    lane = lax.broadcasted_iota(jnp.int32, (B, n), 1)
    row = lax.broadcasted_iota(jnp.int32, (B, n), 0)
    lane_b = lax.broadcasted_iota(jnp.int32, (B, B), 1)
    row_b = lax.broadcasted_iota(jnp.int32, (B, B), 0)

    def step(k, carry):
        at = pl.multiple_of(k * B, B)
        diag = g_ref[pl.ds(at, B), pl.ds(at, B)]
        wk = jnp.concatenate(block_inverse([diag[8 * i : 8 * i + 8] for i in range(B // 8)]), 0)
        wk = jnp.where(lane_b <= row_b, wk, 0.0)
        here = (lane >= at) & (lane < at + B)
        strip = jnp.where(here, jnp.where(lane == row + at, 1.0, 0.0), g_ref[pl.ds(at, B), :])
        y = jnp.dot(wk, strip, precision=HI, preferred_element_type=F32)
        done = jnp.where(lane <= row + at, y, 0.0)
        to = pl.multiple_of(at - first_row, B)
        w_ref[pl.ds(to, B), :] = done
        half_ref[pl.ds(to, B), :] = done.astype(BF16)
        for j in range(blocks[0] + 1, n // B):

            @pl.when(j > k)
            def _():
                old = jnp.where(here, 0.0, g_ref[j * B : (j + 1) * B, :])
                g_ref[j * B : (j + 1) * B, :] = old - lax.dot_general(
                    y[:, j * B : (j + 1) * B],
                    y,
                    (((0,), (0,)), ((), ())),
                    precision=HI,
                    preferred_element_type=F32,
                )

        return carry

    lax.fori_loop(*blocks, step, 0)


def upper_kernel(place_ref, p0, p1, p2, p3, w_ref, half_ref, g_ref):
    for k, piece in enumerate((p0, p1, p2, p3)):
        at = pl.multiple_of((place_ref[0] + 4 - k) % 4 * BLOCK, BLOCK)
        g_ref[pl.ds(at, BLOCK), :] = piece[...].astype(F32)
    whole = g_ref[...]
    g_ref[...] = 0.5 * (whole + whole.T)
    eliminate(g_ref, w_ref, half_ref, (0, 2), 0)


def lower_kernel(in_ref, w_ref, half_ref, g_ref):
    g_ref[in_ref.shape[0] :, :] = in_ref[...]
    eliminate(g_ref, w_ref, half_ref, (2, 4), 2 * BLOCK)


def upper_inverse(pieces, y):
    n = pieces[0].shape[1]
    vmem = pl.BlockSpec(memory_space=pltpu.VMEM)

    def kernel(place_ref, p0, p1, p2, p3, w_ref, half_ref, rest_ref, g_ref):
        upper_kernel(place_ref, p0, p1, p2, p3, w_ref, half_ref, g_ref)
        rest_ref[...] = g_ref[n // 2 :, :]

    return pl.pallas_call(
        kernel,
        out_shape=(
            jax.ShapeDtypeStruct((n // 2, n), F32),
            jax.ShapeDtypeStruct((n // 2, n), BF16),
            jax.ShapeDtypeStruct((n // 2, n), F32),
        ),
        in_specs=[pl.BlockSpec(memory_space=pltpu.SMEM)] + [vmem] * 4,
        out_specs=(vmem,) * 3,
        scratch_shapes=[pltpu.VMEM((n, n), F32)],
        compiler_params=pltpu.CompilerParams(vmem_limit_bytes=16 << 20),
        cost_estimate=pl.CostEstimate(flops=10 << 30, bytes_accessed=4 * n * n, transcendentals=0),
    )(y.reshape(1), *pieces)


def lower_inverse(rest):
    half, n = rest.shape
    vmem = pl.BlockSpec(memory_space=pltpu.VMEM)
    return pl.pallas_call(
        lower_kernel,
        out_shape=(jax.ShapeDtypeStruct((half, n), F32), jax.ShapeDtypeStruct((half, n), BF16)),
        in_specs=[vmem],
        out_specs=(vmem,) * 2,
        scratch_shapes=[pltpu.VMEM((n, n), F32)],
        compiler_params=pltpu.CompilerParams(vmem_limit_bytes=16 << 20),
        cost_estimate=pl.CostEstimate(flops=10 << 30, bytes_accessed=4 * n * n, transcendentals=0),
    )(rest)


def update_kernel(place_ref, pattern_ref, *refs):
    rows_in, first_in, second_in = refs[0:4], refs[4:8], refs[8:12]
    w_top, w_low, half_top, half_low, loads_ref, pivot_ref, trailing_ref, out_ref, loads_out_ref = refs[12:21]
    raw_ref, factor_ref, other_ref, half_ref = refs[21:25]
    n = half_ref.shape[0]
    row_dev = rows_in[0].shape[1]
    tile = out_ref.shape[1]
    step = pl.program_id(0)
    x, y, core, is_owner = place_ref[0], place_ref[1], place_ref[2], place_ref[3]

    def factor_of(pieces, spot, target, column):
        for k, piece in enumerate(pieces):
            at = pl.multiple_of((spot + 4 - k) % 4 * BLOCK, BLOCK)
            raw_ref[pl.ds(at, BLOCK), :] = piece[...]
        for c in range(0, row_dev, 512):
            part = jnp.dot(half_ref[...], raw_ref[:, c : c + 512], preferred_element_type=F32).astype(BF16)
            target[:, pl.ds(pl.multiple_of(column + c, 128), 512)] = part

    @pl.when(step == 0)
    def _():
        half_ref[: n // 2, :] = half_top[...]
        half_ref[n // 2 :, :] = half_low[...]
        factor_of(first_in, x, other_ref, core * row_dev)
        factor_of(second_in, x, other_ref, (1 - core) * row_dev)
        for k, piece in enumerate(rows_in):
            at = pl.multiple_of((y + 4 - k) % 4 * BLOCK, BLOCK)
            raw_ref[pl.ds(at, BLOCK), :] = piece[...]
        for c in range(0, row_dev, 512):
            part = lax.dot_general(
                raw_ref[:, c : c + 512], half_ref[...], (((0,), (1,)), ((), ())), preferred_element_type=F32
            )
            factor_ref[c : c + 512, :] = part.astype(BF16)
        solve = jnp.concatenate(
            [
                lax.dot_general(
                    pivot_ref[...], w[...], (((1,), (1,)), ((), ())), precision=HI, preferred_element_type=F32
                )
                for w in (w_top, w_low)
            ],
            1,
        )
        change = lax.dot_general(
            solve, factor_ref[...].astype(F32), (((1,), (1,)), ((), ())), precision=HI, preferred_element_type=F32
        )
        loads_out_ref[...] = loads_ref[...] - change

        @pl.when(is_owner == 1)
        def _():
            loads_out_ref[:, :n] = solve

    columns = other_ref[:, pl.ds(pl.multiple_of(step * tile, tile), tile)]
    for b in range(0, row_dev, 512):
        product = jnp.dot(factor_ref[b : b + 512, :], columns, preferred_element_type=F32)
        for i in range(0, 512, BLOCK):
            for j in range(0, tile, BLOCK):
                flag = pattern_ref[(b + i) // BLOCK, step * (tile // BLOCK) + j // BLOCK].astype(F32)
                old = trailing_ref[b + i : b + i + BLOCK, j : j + BLOCK].astype(F32)
                new = old - product[i : i + BLOCK, j : j + BLOCK] * flag
                out_ref[b + i : b + i + BLOCK, j : j + BLOCK] = new.astype(BF16)


def update(place, pattern, rows, first, second, w_parts, half_parts, regrouped, pivot_loads, trailing):
    row_dev, col_dev = trailing.shape
    n = half_parts[0].shape[1]
    tile = 256
    smem = pl.BlockSpec(memory_space=pltpu.SMEM)
    vmem = pl.BlockSpec(memory_space=pltpu.VMEM)
    tiled = pl.BlockSpec((row_dev, tile), lambda s: (0, s))
    return pl.pallas_call(
        update_kernel,
        grid=(col_dev // tile,),
        out_shape=(
            jax.ShapeDtypeStruct((row_dev, col_dev), BF16),
            jax.ShapeDtypeStruct((8, row_dev), F32),
        ),
        in_specs=[smem, smem] + [vmem] * 18 + [tiled],
        out_specs=(tiled, vmem),
        scratch_shapes=[
            pltpu.VMEM((n, row_dev), BF16),
            pltpu.VMEM((row_dev, n), BF16),
            pltpu.VMEM((n, col_dev), BF16),
            pltpu.VMEM((n, n), BF16),
        ],
        compiler_params=pltpu.CompilerParams(vmem_limit_bytes=48 << 20),
        cost_estimate=pl.CostEstimate(flops=8 << 30, bytes_accessed=24 << 20, transcendentals=0),
    )(place, pattern, *rows, *first, *second, *w_parts, *half_parts, regrouped, pivot_loads, trailing)


def per_device(loads, nd_source, panel, trailing, pattern, owner):
    row_dev = panel.shape[0]
    row_count = lax.axis_size("row")
    pivot_size = panel.shape[1] * lax.axis_size("col")
    share_size = row_dev // row_count
    row_place = lax.axis_index("row")
    col_place = lax.axis_index("col")
    root = owner[0]
    x, z_hi, core = row_place // 4, row_place // 2 % 2, row_place % 2
    y, z_lo = col_place // 2, col_place % 2
    mine = panel.T

    packet = spread(pack(mine, loads, nd_source), row_place, root)
    head = jnp.concatenate([packet[:24, c * pivot_size : (c + 1) * pivot_size] for c in range(3)], 0)
    pivot = pair_up(head[:64], z_lo, Z_LO, "col")
    moved = lax.ppermute(after(mine, packet), ("row", "col"), transposed_place())
    rows = pair_up(after(mine, packet), z_lo, Z_LO, "col")
    pivot = ring(pivot, Y_SHIFT, "col")
    first = pair_up(after(moved, pivot[0]), z_hi, Z_HI, "row")
    first, rows = after((first, rows), *pivot)
    first = ring(first, X_SHIFT, "row")
    rows = ring(rows, Y_SHIFT, "col")

    everyone = packet[24:].reshape(row_count, 8, row_dev)
    regrouped = regroup(everyone, nd_source, row_place, row_place, share_size)
    pivot_source = head[64].astype(jnp.int32) * BLOCK + head[65].astype(jnp.int32)
    pivot_loads = regroup(everyone, pivot_source, row_place, root, share_size)

    w_top, half_top, rest = upper_inverse(pivot, y)
    second = [lax.ppermute(after(piece, rest), "row", CORE) for piece in first]
    w_low, half_low = lower_inverse(rest)

    place = jnp.stack([x, y, core, (row_place == root).astype(jnp.int32)]).astype(jnp.int32)
    trailing_out, loads_out = update(
        place, pattern, rows, first, second, (w_top, w_low), (half_top, half_low), regrouped, pivot_loads, trailing
    )
    return loads_out[:3], trailing_out


def solution(mesh):
    return jax.shard_map(
        per_device,
        mesh=mesh,
        in_specs=(P(None, "row"), P("row"), P("row", "col"), P("row", "col"), P("row", "col"), P()),
        out_specs=(P(None, "row"), P("row", "col")),
        check_vma=False,
    )
```

```python
import jax
import jax.numpy as jnp
from jax import lax
from jax.experimental import pallas as pl
from jax.experimental.pallas import tpu as pltpu
from jax.sharding import PartitionSpec as P

HI = lax.Precision.HIGHEST
F32 = jnp.float32
BF16 = jnp.bfloat16
BLOCK = 128

X_SHIFT = {k: [(i, (i // 4 + k) % 4 * 4 + i % 4) for i in range(16)] for k in (1, 2, 3)}
Y_SHIFT = {k: [(i, (i // 2 + k) % 4 * 2 + i % 2) for i in range(8)] for k in (1, 2, 3)}
Z_HI = [(i, i ^ 2) for i in range(16)]
CORE = [(i, i ^ 1) for i in range(16)]
Z_LO = [(i, i ^ 1) for i in range(8)]


def transposed_place():
    pairs = []
    for row in range(16):
        for col in range(8):
            x, z_hi, core = row // 4, row // 2 % 2, row % 2
            y, z_lo = col // 2, col % 2
            pairs.append((row * 8 + col, ((y * 2 + z_lo) * 2 + core) * 8 + x * 2 + z_hi))
    return pairs


def ring(mine, shifts, axis):
    return [mine] + [lax.ppermute(mine, axis, shifts[k]) for k in (1, 2, 3)]


def pack_kernel(panel_ref, loads_ref, source_ref, out_ref):
    size = out_ref.shape[1] // 3
    source = jnp.concatenate([source_ref[k : k + 1, :] for k in range(size // BLOCK)], 1)
    digits = jnp.concatenate([source // BLOCK, source % BLOCK, jnp.zeros((6, size), jnp.int32)], 0)
    head = jnp.concatenate([panel_ref[:, :size].astype(F32), digits.astype(F32)], 0)
    head = jnp.concatenate([head[24 * c : 24 * c + 24] for c in range(3)], 1)
    loads = loads_ref[...]
    high = loads.astype(BF16).astype(F32)
    low = loads - high
    tail = jnp.concatenate([high, low, jnp.zeros((2, loads.shape[1]), F32)], 0)
    out_ref[...] = jnp.concatenate([head, tail], 0).astype(BF16)


def pack(mine, loads, source):
    return pl.pallas_call(
        pack_kernel,
        out_shape=jax.ShapeDtypeStruct((32, mine.shape[1]), BF16),
        compiler_params=pltpu.CompilerParams(vmem_limit_bytes=4 << 20),
    )(mine, loads, source.reshape(-1, BLOCK))


def small_call(kernel, shapes, scalars, *arrays):
    vmem = pl.BlockSpec(memory_space=pltpu.VMEM)
    return pl.pallas_call(
        kernel,
        out_shape=tuple(jax.ShapeDtypeStruct(shape, BF16) for shape in shapes),
        in_specs=[pl.BlockSpec(memory_space=pltpu.SMEM)] + [vmem] * len(arrays),
        out_specs=(vmem,) * len(shapes),
        compiler_params=pltpu.CompilerParams(vmem_limit_bytes=4 << 20),
    )(scalars, *arrays)


def choose_x(at_ref, p0, p1, p2, p3, out_ref):
    back = ((at_ref[0] >> 2) + 4 - (at_ref[2] >> 2)) & 3
    pieces = [p[...].astype(F32) for p in (p0, p1, p2, p3)]
    head = pieces[0][:24]
    for k in (1, 2, 3):
        head = jnp.where(back == k, pieces[k][:24], head)
    out_ref[...] = jnp.concatenate([head] + [p[24:] for p in pieces], 0).astype(BF16)


def choose_z(at_ref, p0, p1, out_ref):
    own, other = p0[...].astype(F32), p1[...].astype(F32)
    head = jnp.where(((at_ref[0] ^ at_ref[2]) & 2) == 0, own[:24], other[:24])
    out_ref[...] = jnp.concatenate([head, own[24:], other[24:]], 0).astype(BF16)


def choose_core(at_ref, p0, p1, pivot_ref, digits_ref):
    size = pivot_ref.shape[1]
    head = jnp.where(((at_ref[0] ^ at_ref[2]) & 1) == 0, p0[...].astype(F32)[:24], p1[...].astype(F32)[:24])
    head = jnp.concatenate([head[:, c * size : (c + 1) * size] for c in range(3)], 0)
    pivot_ref[...] = head[:64].astype(BF16)
    digits_ref[...] = head[64:].astype(BF16)


def pair_z_lo(at_ref, p0, p1, out_ref):
    own, other = p0[...], p1[...]
    low = (at_ref[1] & 1) == 0
    out_ref[...] = jnp.concatenate([jnp.where(low, own, other), jnp.where(low, other, own)], 0)


def pair_z_hi(at_ref, p0, p1, out_ref):
    own, other = p0[...], p1[...]
    low = (at_ref[0] & 2) == 0
    out_ref[...] = jnp.concatenate([jnp.where(low, own, other), jnp.where(low, other, own)], 0)


def regroup(window_of, source, row_place, target, share):
    arrived = lax.dynamic_slice_in_dim(window_of, target * share, share, 2)
    arrived = arrived.transpose(1, 0, 2).reshape(arrived.shape[1], -1)
    home = lax.div(source, share * 16)
    flip = home ^ row_place
    turn = ((row_place >> 2) + 4 - (home >> 2)) & 3
    place = (flip & 1) * 8 + (flip & 2) * 2 + turn
    slot = (place - home * 16) * share + source - target * share
    parts = jnp.take(arrived, slot, axis=1)
    return jnp.concatenate([parts[:3].astype(F32) + parts[3:6].astype(F32), jnp.zeros((5, slot.shape[0]), F32)], 0)


def block_inverse(rows):
    n = rows[0].shape[1]
    lane = lax.broadcasted_iota(jnp.int32, (8, n), 1)
    sub = lax.broadcasted_iota(jnp.int32, (8, n), 0)
    rows = list(rows)
    out = []
    for g in range(len(rows)):
        p = 8 * g
        below = range(g + 1, len(rows))
        strip = rows[g]
        cols = [jnp.broadcast_to(strip[:, p + k : p + k + 1], (8, n)) for k in range(8)]
        cols_below = {
            i: [jnp.broadcast_to(rows[i][:, p + k : p + k + 1], (8, n)) for k in range(8)] for i in below
        }
        in_block = (lane >= p) & (lane < p + 8)
        for i in below:
            rows[i] = jnp.where(in_block, 0.0, rows[i])
        pivots = None
        for k in range(8):
            d = jnp.broadcast_to(cols[k][k : k + 1, :], (8, n))
            r = 1.0 / d
            pivots = d if k == 0 else jnp.where(sub == k, d, pivots)
            m = jnp.where(sub > k, cols[k] * r, 0.0)
            piv = jnp.where(lane == p + k, 1.0, jnp.broadcast_to(strip[k : k + 1, :], (8, n)))
            strip = jnp.where((lane == p + k) & (sub > k), 0.0, strip) - m * piv
            piv = jnp.where((lane > p + k) & (lane < p + 8), 0.0, piv)
            u = [None] * 8
            for q in range(k + 1, 8):
                u[q] = jnp.broadcast_to(cols[q][k : k + 1, :], (8, n))
                cols[q] = cols[q] - m * u[q]
            for i in below:
                f = cols_below[i][k] * r
                for q in range(k + 1, 8):
                    cols_below[i][q] = cols_below[i][q] - f * u[q]
                rows[i] = rows[i] - f * piv
        s = lax.rsqrt(pivots)
        out.append(jnp.where(lane == sub + p, s, strip * s))
    return out


def eliminate(g_ref, w_ref, half_ref, blocks, first_row):
    n = g_ref.shape[0]
    B = BLOCK
    lane = lax.broadcasted_iota(jnp.int32, (B, n), 1)
    row = lax.broadcasted_iota(jnp.int32, (B, n), 0)
    lane_b = lax.broadcasted_iota(jnp.int32, (B, B), 1)
    row_b = lax.broadcasted_iota(jnp.int32, (B, B), 0)

    def step(k, carry):
        at = pl.multiple_of(k * B, B)
        diag = g_ref[pl.ds(at, B), pl.ds(at, B)]
        wk = jnp.concatenate(block_inverse([diag[8 * i : 8 * i + 8] for i in range(B // 8)]), 0)
        wk = jnp.where(lane_b <= row_b, wk, 0.0)
        here = (lane >= at) & (lane < at + B)
        strip = jnp.where(here, jnp.where(lane == row + at, 1.0, 0.0), g_ref[pl.ds(at, B), :])
        y = jnp.dot(wk, strip, precision=HI, preferred_element_type=F32)
        done = jnp.where(lane <= row + at, y, 0.0)
        to = pl.multiple_of(at - first_row, B)
        w_ref[pl.ds(to, B), :] = done
        half_ref[pl.ds(to, B), :] = done.astype(BF16)
        for j in range(blocks[0] + 1, n // B):

            @pl.when(j > k)
            def _():
                old = jnp.where(here, 0.0, g_ref[j * B : (j + 1) * B, :])
                g_ref[j * B : (j + 1) * B, :] = old - lax.dot_general(
                    y[:, j * B : (j + 1) * B],
                    y,
                    (((0,), (0,)), ((), ())),
                    precision=HI,
                    preferred_element_type=F32,
                )

        return carry

    lax.fori_loop(*blocks, step, 0)


def upper_kernel(at_ref, p0, p1, p2, p3, w_ref, half_ref, g_ref):
    for k, piece in enumerate((p0, p1, p2, p3)):
        at = pl.multiple_of((((at_ref[1] >> 1) + 4 - k) & 3) * BLOCK, BLOCK)
        g_ref[pl.ds(at, BLOCK), :] = piece[...].astype(F32)
    whole = g_ref[...]
    g_ref[...] = 0.5 * (whole + whole.T)
    eliminate(g_ref, w_ref, half_ref, (0, 2), 0)


def lower_kernel(in_ref, w_ref, half_ref, g_ref):
    g_ref[in_ref.shape[0] :, :] = in_ref[...]
    eliminate(g_ref, w_ref, half_ref, (2, 4), 2 * BLOCK)


def upper_inverse(pieces, at):
    n = pieces[0].shape[1]
    vmem = pl.BlockSpec(memory_space=pltpu.VMEM)

    def kernel(at_ref, p0, p1, p2, p3, w_ref, half_ref, rest_ref, g_ref):
        upper_kernel(at_ref, p0, p1, p2, p3, w_ref, half_ref, g_ref)
        rest_ref[...] = g_ref[n // 2 :, :]

    return pl.pallas_call(
        kernel,
        out_shape=(
            jax.ShapeDtypeStruct((n // 2, n), F32),
            jax.ShapeDtypeStruct((n // 2, n), BF16),
            jax.ShapeDtypeStruct((n // 2, n), F32),
        ),
        in_specs=[pl.BlockSpec(memory_space=pltpu.SMEM)] + [vmem] * 4,
        out_specs=(vmem,) * 3,
        scratch_shapes=[pltpu.VMEM((n, n), F32)],
        compiler_params=pltpu.CompilerParams(vmem_limit_bytes=8 << 20),
        cost_estimate=pl.CostEstimate(flops=10 << 30, bytes_accessed=4 * n * n, transcendentals=0),
    )(at, *pieces)


def lower_inverse(rest):
    half, n = rest.shape
    vmem = pl.BlockSpec(memory_space=pltpu.VMEM)
    return pl.pallas_call(
        lower_kernel,
        out_shape=(jax.ShapeDtypeStruct((half, n), F32), jax.ShapeDtypeStruct((half, n), BF16)),
        in_specs=[vmem],
        out_specs=(vmem,) * 2,
        scratch_shapes=[pltpu.VMEM((n, n), F32)],
        compiler_params=pltpu.CompilerParams(vmem_limit_bytes=8 << 20),
        cost_estimate=pl.CostEstimate(flops=10 << 30, bytes_accessed=4 * n * n, transcendentals=0),
    )(rest)


def update_kernel(at_ref, pattern_ref, *refs):
    rows_in, first_in, second_in = refs[0:4], refs[4:8], refs[8:12]
    w_top, w_low, half_top, half_low, loads_ref, pivot_ref, trailing_ref, out_ref, loads_out_ref = refs[12:21]
    factor_ref, other_ref, half_ref, new_ref, list_ref, sems = refs[21:27]
    raw_refs = refs[27:30]
    n = half_ref.shape[0]
    row_dev, col_dev = trailing_ref.shape
    x, y, core = at_ref[0] >> 2, at_ref[1] >> 1, at_ref[0] & 1

    def copy(source, s):
        at = pl.ds(pl.multiple_of(s * BLOCK, BLOCK), BLOCK)
        return pltpu.make_async_copy(source.at[at, :], out_ref.at[at, :], sems.at[s])

    def sort_strip(s, count):
        filled = pattern_ref[s, 0]
        for j in range(1, col_dev // BLOCK):
            filled = filled | pattern_ref[s, j]

        @pl.when(filled != 0)
        def _():
            list_ref[count] = s

        @pl.when(filled == 0)
        def _():
            copy(trailing_ref, s).start()

        return count + (filled != 0).astype(jnp.int32)

    count = lax.fori_loop(0, row_dev // BLOCK, sort_strip, 0)
    half_ref[: n // 2, :] = half_top[...]
    half_ref[n // 2 :, :] = half_low[...]

    def assemble(raw_ref, pieces, spot):
        for k, piece in enumerate(pieces):
            at = pl.multiple_of(((spot + 4 - k) & 3) * BLOCK, BLOCK)
            raw_ref[pl.ds(at, BLOCK), :] = piece[...]

    assemble(raw_refs[0], rows_in, y)
    assemble(raw_refs[1], first_in, x)
    assemble(raw_refs[2], second_in, x)
    for c in range(0, row_dev, 512):
        part = lax.dot_general(
            raw_refs[0][:, c : c + 512], half_ref[...], (((0,), (1,)), ((), ())), preferred_element_type=F32
        )
        factor_ref[c : c + 512, :] = part.astype(BF16)
    for raw_ref, column in ((raw_refs[1], core * row_dev), (raw_refs[2], (1 - core) * row_dev)):
        for c in range(0, row_dev, 512):
            part = jnp.dot(half_ref[...], raw_ref[:, c : c + 512], preferred_element_type=F32).astype(BF16)
            other_ref[:, pl.ds(pl.multiple_of(column + c, 128), 512)] = part

    TILE = 512

    def strip_at(s):
        return pl.ds(pl.multiple_of(s * BLOCK, BLOCK), BLOCK)

    def pair_step(p, carry):
        last = 2 * p + 1 < count
        pair = (list_ref[2 * p], list_ref[jnp.where(last, 2 * p + 1, 2 * p)])
        left = jnp.concatenate([factor_ref[strip_at(s), :] for s in pair], 0)
        for t in range(0, col_dev, TILE):
            product = jnp.dot(left, other_ref[:, t : t + TILE], preferred_element_type=F32)
            for i, s in enumerate(pair):
                for j in range(0, TILE, BLOCK):
                    flag = pattern_ref[s, (t + j) // BLOCK].astype(F32)
                    old = trailing_ref[strip_at(s), t + j : t + j + BLOCK].astype(F32)
                    new = old - product[i * BLOCK : (i + 1) * BLOCK, j : j + BLOCK] * flag
                    new_ref[strip_at(s), t + j : t + j + BLOCK] = new.astype(BF16)
        copy(new_ref, pair[0]).start()

        @pl.when(last)
        def _():
            copy(new_ref, pair[1]).start()

        return carry

    lax.fori_loop(0, (count + 1) // 2, pair_step, 0)

    solve = jnp.concatenate(
        [
            lax.dot_general(
                pivot_ref[...], w[...], (((1,), (1,)), ((), ())), precision=HI, preferred_element_type=F32
            )
            for w in (w_top, w_low)
        ],
        1,
    )
    one = solve.astype(BF16)
    rest = solve - one.astype(F32)
    two = rest.astype(BF16)
    three = (rest - two.astype(F32)).astype(BF16)
    parts = jnp.concatenate([p.astype(F32) for p in (one, two, three)], 0).astype(BF16)
    change = lax.dot_general(parts, factor_ref[...], (((1,), (1,)), ((), ())), preferred_element_type=F32)
    loads_out_ref[...] = (loads_ref[...] - (change[:8] + change[8:16] + change[16:24]))[:3]

    @pl.when(at_ref[0] == at_ref[2])
    def _():
        loads_out_ref[:, :n] = solve[:3]

    lax.fori_loop(0, row_dev // BLOCK, lambda s, c: (copy(new_ref, s).wait(), c)[1], 0)


def update(at, pattern, rows, first, second, w_parts, half_parts, regrouped, pivot_loads, trailing):
    row_dev, col_dev = trailing.shape
    n = half_parts[0].shape[1]
    smem = pl.BlockSpec(memory_space=pltpu.SMEM)
    vmem = pl.BlockSpec(memory_space=pltpu.VMEM)
    return pl.pallas_call(
        update_kernel,
        out_shape=(
            jax.ShapeDtypeStruct((row_dev, col_dev), BF16),
            jax.ShapeDtypeStruct((3, row_dev), F32),
        ),
        in_specs=[smem, smem] + [vmem] * 19,
        out_specs=(pl.BlockSpec(memory_space=pl.ANY), vmem),
        scratch_shapes=[
            pltpu.VMEM((row_dev, n), BF16),
            pltpu.VMEM((n, col_dev), BF16),
            pltpu.VMEM((n, n), BF16),
            pltpu.VMEM((row_dev, col_dev), BF16),
            pltpu.SMEM((row_dev // BLOCK,), jnp.int32),
            pltpu.SemaphoreType.DMA((row_dev // BLOCK,)),
        ]
        + [pltpu.VMEM((n, row_dev), BF16)] * 3,
        compiler_params=pltpu.CompilerParams(vmem_limit_bytes=28 << 20),
        cost_estimate=pl.CostEstimate(flops=8 << 30, bytes_accessed=24 << 20, transcendentals=0),
    )(at, pattern, *rows, *first, *second, *w_parts, *half_parts, regrouped, pivot_loads, trailing)


def per_device(loads, nd_source, panel, trailing, pattern, owner):
    row_dev = panel.shape[0]
    row_count = lax.axis_size("row")
    slice_width = panel.shape[1]
    pivot_size = slice_width * lax.axis_size("col")
    share_size = row_dev // row_count
    row_place = lax.axis_index("row")
    root = owner[0]
    at = jnp.stack([row_place, lax.axis_index("col"), root])
    mine = panel.T
    both = lax.optimization_barrier

    packets = ring(pack(mine, loads, nd_source), X_SHIFT, "row")
    rows_other = lax.ppermute(mine, "col", Z_LO)
    (packet,) = small_call(choose_x, [(56, row_dev)], at, *packets)
    packet, moving = both((packet, mine))
    packet_other = lax.ppermute(packet, "row", Z_HI)
    moved = lax.ppermute(moving, ("row", "col"), transposed_place())
    (packet,) = small_call(choose_z, [(88, row_dev)], at, packet, packet_other)
    packet_other = lax.ppermute(packet, "row", CORE)
    pivot, digits = small_call(
        choose_core, [(slice_width, pivot_size), (8, pivot_size)], at, packet, packet_other
    )
    pivot, moved = both((pivot, moved))
    pivot_other = lax.ppermute(pivot, "col", Z_LO)
    moved_other = lax.ppermute(moved, "row", Z_HI)
    (pivot,) = small_call(pair_z_lo, [(2 * slice_width, pivot_size)], at, pivot, pivot_other)
    (rows,) = small_call(pair_z_lo, [(2 * slice_width, row_dev)], at, mine, rows_other)
    pivot = ring(pivot, Y_SHIFT, "col")
    (first,) = small_call(pair_z_hi, [(2 * slice_width, row_dev)], at, moved, moved_other)
    first = ring(first, X_SHIFT, "row")
    pivot, rows = both((pivot, rows))
    rows = ring(rows, Y_SHIFT, "col")

    w_top, half_top, rest = upper_inverse(pivot, at)
    rest, first, packet, packet_other = both((rest, first, packet, packet_other))
    second = [lax.ppermute(piece, "row", CORE) for piece in first]

    everyone = jnp.concatenate([packet[24:], packet_other[24:]], 0).reshape(row_count, 8, row_dev)
    regrouped = regroup(everyone, nd_source, row_place, row_place, share_size)
    pivot_source = digits[0].astype(jnp.int32) * BLOCK + digits[1].astype(jnp.int32)
    pivot_loads = regroup(everyone, pivot_source, row_place, root, share_size)

    rest, regrouped, pivot_loads = both((rest, regrouped, pivot_loads))
    w_low, half_low = lower_inverse(rest)
    trailing_out, loads_out = update(
        at, pattern, rows, first, second, (w_top, w_low), (half_top, half_low), regrouped, pivot_loads, trailing
    )
    return loads_out, trailing_out


def solution(mesh):
    return jax.shard_map(
        per_device,
        mesh=mesh,
        in_specs=(P(None, "row"), P("row"), P("row", "col"), P("row", "col"), P("row", "col"), P()),
        out_specs=(P(None, "row"), P("row", "col")),
        check_vma=False,
    )
```

```python
import jax
import jax.numpy as jnp
from jax import lax
from jax.experimental import pallas as pl
from jax.experimental.pallas import tpu as pltpu
from jax.sharding import PartitionSpec as P

HI = lax.Precision.HIGHEST
F32 = jnp.float32
BF16 = jnp.bfloat16
BLOCK = 128

X_SHIFT = {k: [(i, (i // 4 + k) % 4 * 4 + i % 4) for i in range(16)] for k in (1, 2, 3)}
Y_SHIFT = {k: [(i, (i // 2 + k) % 4 * 2 + i % 2) for i in range(8)] for k in (1, 2, 3)}
Z_HI = [(i, i ^ 2) for i in range(16)]
CORE = [(i, i ^ 1) for i in range(16)]
Z_LO = [(i, i ^ 1) for i in range(8)]


def transposed_place():
    pairs = []
    for row in range(16):
        for col in range(8):
            x, z_hi, core = row // 4, row // 2 % 2, row % 2
            y, z_lo = col // 2, col % 2
            pairs.append((row * 8 + col, ((y * 2 + z_lo) * 2 + core) * 8 + x * 2 + z_hi))
    return pairs


def ring(mine, shifts, axis):
    return [mine] + [lax.ppermute(mine, axis, shifts[k]) for k in (1, 2, 3)]


def pack_kernel(panel_ref, loads_ref, source_ref, out_ref):
    size = out_ref.shape[1] // 3
    source = jnp.concatenate([source_ref[k : k + 1, :] for k in range(size // BLOCK)], 1)
    digits = jnp.concatenate([source // BLOCK, source % BLOCK, jnp.zeros((6, size), jnp.int32)], 0)
    head = jnp.concatenate([panel_ref[:, :size].astype(F32), digits.astype(F32)], 0)
    head = jnp.concatenate([head[24 * c : 24 * c + 24] for c in range(3)], 1)
    loads = loads_ref[...]
    high = loads.astype(BF16).astype(F32)
    low = loads - high
    tail = jnp.concatenate([high, low, jnp.zeros((2, loads.shape[1]), F32)], 0)
    out_ref[...] = jnp.concatenate([head, tail], 0).astype(BF16)


def pack(mine, loads, source):
    return pl.pallas_call(
        pack_kernel,
        out_shape=jax.ShapeDtypeStruct((32, mine.shape[1]), BF16),
        compiler_params=pltpu.CompilerParams(vmem_limit_bytes=4 << 20),
    )(mine, loads, source.reshape(-1, BLOCK))


def small_call(kernel, shapes, scalars, *arrays):
    vmem = pl.BlockSpec(memory_space=pltpu.VMEM)
    return pl.pallas_call(
        kernel,
        out_shape=tuple(jax.ShapeDtypeStruct(shape, BF16) for shape in shapes),
        in_specs=[pl.BlockSpec(memory_space=pltpu.SMEM)] + [vmem] * len(arrays),
        out_specs=(vmem,) * len(shapes),
        compiler_params=pltpu.CompilerParams(vmem_limit_bytes=4 << 20),
    )(scalars, *arrays)


def choose_x(at_ref, p0, p1, p2, p3, out_ref):
    back = ((at_ref[0] >> 2) + 4 - (at_ref[2] >> 2)) & 3
    pieces = [p[...].astype(F32) for p in (p0, p1, p2, p3)]
    head = pieces[0][:24]
    for k in (1, 2, 3):
        head = jnp.where(back == k, pieces[k][:24], head)
    out_ref[...] = jnp.concatenate([head] + [p[24:] for p in pieces], 0).astype(BF16)


def choose_z(at_ref, p0, p1, out_ref):
    own, other = p0[...].astype(F32), p1[...].astype(F32)
    head = jnp.where(((at_ref[0] ^ at_ref[2]) & 2) == 0, own[:24], other[:24])
    out_ref[...] = jnp.concatenate([head, own[24:], other[24:]], 0).astype(BF16)


def choose_core(at_ref, p0, p1, pivot_ref, digits_ref):
    size = pivot_ref.shape[1]
    head = jnp.where(((at_ref[0] ^ at_ref[2]) & 1) == 0, p0[...].astype(F32)[:24], p1[...].astype(F32)[:24])
    head = jnp.concatenate([head[:, c * size : (c + 1) * size] for c in range(3)], 0)
    pivot_ref[...] = head[:64].astype(BF16)
    digits_ref[...] = head[64:].astype(BF16)


def pair_z_lo(at_ref, p0, p1, out_ref):
    own, other = p0[...], p1[...]
    low = (at_ref[1] & 1) == 0
    out_ref[...] = jnp.concatenate([jnp.where(low, own, other), jnp.where(low, other, own)], 0)


def pair_z_hi(at_ref, p0, p1, out_ref):
    own, other = p0[...], p1[...]
    low = (at_ref[0] & 2) == 0
    out_ref[...] = jnp.concatenate([jnp.where(low, own, other), jnp.where(low, other, own)], 0)


def regroup(window_of, source, row_place, target, share):
    arrived = lax.dynamic_slice_in_dim(window_of, target * share, share, 2)
    arrived = arrived.transpose(1, 0, 2).reshape(arrived.shape[1], -1)
    home = lax.div(source, share * 16)
    flip = home ^ row_place
    turn = ((row_place >> 2) + 4 - (home >> 2)) & 3
    place = (flip & 1) * 8 + (flip & 2) * 2 + turn
    slot = (place - home * 16) * share + source - target * share
    parts = jnp.take(arrived, slot, axis=1)
    return jnp.concatenate([parts[:3].astype(F32) + parts[3:6].astype(F32), jnp.zeros((5, slot.shape[0]), F32)], 0)


def block_inverse(rows):
    n = rows[0].shape[1]
    lane = lax.broadcasted_iota(jnp.int32, (8, n), 1)
    sub = lax.broadcasted_iota(jnp.int32, (8, n), 0)
    rows = list(rows)
    out = []
    for g in range(len(rows)):
        p = 8 * g
        below = range(g + 1, len(rows))
        strip = rows[g]
        cols = [jnp.broadcast_to(strip[:, p + k : p + k + 1], (8, n)) for k in range(8)]
        cols_below = {
            i: [jnp.broadcast_to(rows[i][:, p + k : p + k + 1], (8, n)) for k in range(8)] for i in below
        }
        in_block = (lane >= p) & (lane < p + 8)
        for i in below:
            rows[i] = jnp.where(in_block, 0.0, rows[i])
        pivots = None
        for k in range(8):
            d = jnp.broadcast_to(cols[k][k : k + 1, :], (8, n))
            r = 1.0 / d
            pivots = d if k == 0 else jnp.where(sub == k, d, pivots)
            m = jnp.where(sub > k, cols[k] * r, 0.0)
            piv = jnp.where(lane == p + k, 1.0, jnp.broadcast_to(strip[k : k + 1, :], (8, n)))
            strip = jnp.where((lane == p + k) & (sub > k), 0.0, strip) - m * piv
            piv = jnp.where((lane > p + k) & (lane < p + 8), 0.0, piv)
            u = [None] * 8
            for q in range(k + 1, 8):
                u[q] = jnp.broadcast_to(cols[q][k : k + 1, :], (8, n))
                cols[q] = cols[q] - m * u[q]
            for i in below:
                f = cols_below[i][k] * r
                for q in range(k + 1, 8):
                    cols_below[i][q] = cols_below[i][q] - f * u[q]
                rows[i] = rows[i] - f * piv
        s = lax.rsqrt(pivots)
        out.append(jnp.where(lane == sub + p, s, strip * s))
    return out


def eliminate(g_ref, w_ref, half_ref, blocks, first_row):
    n = g_ref.shape[0]
    B = BLOCK
    lane = lax.broadcasted_iota(jnp.int32, (B, n), 1)
    row = lax.broadcasted_iota(jnp.int32, (B, n), 0)
    lane_b = lax.broadcasted_iota(jnp.int32, (B, B), 1)
    row_b = lax.broadcasted_iota(jnp.int32, (B, B), 0)

    def step(k, carry):
        at = pl.multiple_of(k * B, B)
        diag = g_ref[pl.ds(at, B), pl.ds(at, B)]
        wk = jnp.concatenate(block_inverse([diag[8 * i : 8 * i + 8] for i in range(B // 8)]), 0)
        wk = jnp.where(lane_b <= row_b, wk, 0.0)
        here = (lane >= at) & (lane < at + B)
        strip = jnp.where(here, jnp.where(lane == row + at, 1.0, 0.0), g_ref[pl.ds(at, B), :])
        y = jnp.dot(wk, strip, precision=HI, preferred_element_type=F32)
        done = jnp.where(lane <= row + at, y, 0.0)
        to = pl.multiple_of(at - first_row, B)
        w_ref[pl.ds(to, B), :] = done
        half_ref[pl.ds(to, B), :] = done.astype(BF16)
        for j in range(blocks[0] + 1, n // B):

            @pl.when(j > k)
            def _():
                old = jnp.where(here, 0.0, g_ref[j * B : (j + 1) * B, :])
                g_ref[j * B : (j + 1) * B, :] = old - lax.dot_general(
                    y[:, j * B : (j + 1) * B],
                    y,
                    (((0,), (0,)), ((), ())),
                    precision=HI,
                    preferred_element_type=F32,
                )

        return carry

    lax.fori_loop(*blocks, step, 0)


def upper_kernel(at_ref, p0, p1, p2, p3, w_ref, half_ref, g_ref):
    for k, piece in enumerate((p0, p1, p2, p3)):
        at = pl.multiple_of((((at_ref[1] >> 1) + 4 - k) & 3) * BLOCK, BLOCK)
        g_ref[pl.ds(at, BLOCK), :] = piece[...].astype(F32)
    whole = g_ref[...]
    g_ref[...] = 0.5 * (whole + whole.T)
    eliminate(g_ref, w_ref, half_ref, (0, 2), 0)


def lower_kernel(in_ref, w_top, half_top, w_ref, half_ref, g_ref):
    top = in_ref.shape[0]
    g_ref[top:, :] = in_ref[...]
    w_ref[:top, :] = w_top[...]
    half_ref[:top, :] = half_top[...]
    eliminate(g_ref, w_ref, half_ref, (2, 4), 0)


def upper_inverse(pieces, at):
    n = pieces[0].shape[1]
    vmem = pl.BlockSpec(memory_space=pltpu.VMEM)

    def kernel(at_ref, p0, p1, p2, p3, w_ref, half_ref, rest_ref, g_ref):
        upper_kernel(at_ref, p0, p1, p2, p3, w_ref, half_ref, g_ref)
        rest_ref[...] = g_ref[n // 2 :, :]

    return pl.pallas_call(
        kernel,
        out_shape=(
            jax.ShapeDtypeStruct((n // 2, n), F32),
            jax.ShapeDtypeStruct((n // 2, n), BF16),
            jax.ShapeDtypeStruct((n // 2, n), F32),
        ),
        in_specs=[pl.BlockSpec(memory_space=pltpu.SMEM)] + [vmem] * 4,
        out_specs=(vmem,) * 3,
        scratch_shapes=[pltpu.VMEM((n, n), F32)],
        compiler_params=pltpu.CompilerParams(vmem_limit_bytes=8 << 20),
        cost_estimate=pl.CostEstimate(flops=10 << 30, bytes_accessed=4 * n * n, transcendentals=0),
    )(at, *pieces)


def lower_inverse(rest, w_top, half_top):
    n = rest.shape[1]
    vmem = pl.BlockSpec(memory_space=pltpu.VMEM)
    return pl.pallas_call(
        lower_kernel,
        out_shape=(jax.ShapeDtypeStruct((n, n), F32), jax.ShapeDtypeStruct((n, n), BF16)),
        in_specs=[vmem] * 3,
        out_specs=(vmem,) * 2,
        scratch_shapes=[pltpu.VMEM((n, n), F32)],
        compiler_params=pltpu.CompilerParams(vmem_limit_bytes=8 << 20),
        cost_estimate=pl.CostEstimate(flops=10 << 30, bytes_accessed=4 * n * n, transcendentals=0),
    )(rest, w_top, half_top)


def update_kernel(at_ref, pattern_ref, *refs):
    rows_in, first_in, second_in = refs[0:4], refs[4:8], refs[8:12]
    w_ref, half_ref, loads_ref, pivot_ref, trailing_ref, out_ref, loads_out_ref = refs[12:19]
    factor_ref, other_ref, new_ref, list_ref, sems = refs[19:24]
    raw_refs = refs[24:27]
    n = half_ref.shape[0]
    row_dev, col_dev = trailing_ref.shape
    x, y, core = at_ref[0] >> 2, at_ref[1] >> 1, at_ref[0] & 1

    def copy(source, s):
        at = pl.ds(pl.multiple_of(s * BLOCK, BLOCK), BLOCK)
        return pltpu.make_async_copy(source.at[at, :], out_ref.at[at, :], sems.at[s])

    def sort_strip(s, count):
        filled = pattern_ref[s, 0]
        for j in range(1, col_dev // BLOCK):
            filled = filled | pattern_ref[s, j]

        @pl.when(filled != 0)
        def _():
            list_ref[count] = s

        @pl.when(filled == 0)
        def _():
            copy(trailing_ref, s).start()

        return count + (filled != 0).astype(jnp.int32)

    count = lax.fori_loop(0, row_dev // BLOCK, sort_strip, 0)

    def assemble(raw_ref, pieces, spot):
        for k, piece in enumerate(pieces):
            at = pl.multiple_of(((spot + 4 - k) & 3) * BLOCK, BLOCK)
            raw_ref[pl.ds(at, BLOCK), :] = piece[...]

    assemble(raw_refs[0], rows_in, y)
    assemble(raw_refs[1], first_in, x)
    assemble(raw_refs[2], second_in, x)
    for c in range(0, row_dev, 512):
        part = lax.dot_general(
            raw_refs[0][:, c : c + 512], half_ref[...], (((0,), (1,)), ((), ())), preferred_element_type=F32
        )
        factor_ref[c : c + 512, :] = part.astype(BF16)
    for raw_ref, column in ((raw_refs[1], core * row_dev), (raw_refs[2], (1 - core) * row_dev)):
        for c in range(0, row_dev, 512):
            part = jnp.dot(half_ref[...], raw_ref[:, c : c + 512], preferred_element_type=F32).astype(BF16)
            other_ref[:, pl.ds(pl.multiple_of(column + c, 128), 512)] = part

    TILE = 512

    def strip_at(s):
        return pl.ds(pl.multiple_of(s * BLOCK, BLOCK), BLOCK)

    def pair_step(p, carry):
        last = 2 * p + 1 < count
        pair = (list_ref[2 * p], list_ref[jnp.where(last, 2 * p + 1, 2 * p)])
        left = jnp.concatenate([factor_ref[strip_at(s), :] for s in pair], 0)
        for t in range(0, col_dev, TILE):
            product = jnp.dot(left, other_ref[:, t : t + TILE], preferred_element_type=F32)
            for i, s in enumerate(pair):
                for j in range(0, TILE, BLOCK):
                    flag = pattern_ref[s, (t + j) // BLOCK].astype(F32)
                    old = trailing_ref[strip_at(s), t + j : t + j + BLOCK].astype(F32)
                    new = old - product[i * BLOCK : (i + 1) * BLOCK, j : j + BLOCK] * flag
                    new_ref[strip_at(s), t + j : t + j + BLOCK] = new.astype(BF16)
        copy(new_ref, pair[0]).start()

        @pl.when(last)
        def _():
            copy(new_ref, pair[1]).start()

        return carry

    lax.fori_loop(0, (count + 1) // 2, pair_step, 0)

    solve = lax.dot_general(
        pivot_ref[...], w_ref[...], (((1,), (1,)), ((), ())), precision=HI, preferred_element_type=F32
    )
    one = solve.astype(BF16)
    rest = solve - one.astype(F32)
    two = rest.astype(BF16)
    three = (rest - two.astype(F32)).astype(BF16)
    parts = jnp.concatenate([p.astype(F32) for p in (one, two, three)], 0).astype(BF16)
    change = lax.dot_general(parts, factor_ref[...], (((1,), (1,)), ((), ())), preferred_element_type=F32)
    loads_out_ref[...] = (loads_ref[...] - (change[:8] + change[8:16] + change[16:24]))[:3]

    @pl.when(at_ref[0] == at_ref[2])
    def _():
        loads_out_ref[:, :n] = solve[:3]

    lax.fori_loop(0, row_dev // BLOCK, lambda s, c: (copy(new_ref, s).wait(), c)[1], 0)


def update(at, pattern, rows, first, second, w, half, regrouped, pivot_loads, trailing):
    row_dev, col_dev = trailing.shape
    n = half.shape[0]
    smem = pl.BlockSpec(memory_space=pltpu.SMEM)
    vmem = pl.BlockSpec(memory_space=pltpu.VMEM)
    return pl.pallas_call(
        update_kernel,
        out_shape=(
            jax.ShapeDtypeStruct((row_dev, col_dev), BF16),
            jax.ShapeDtypeStruct((3, row_dev), F32),
        ),
        in_specs=[smem, smem] + [vmem] * 17,
        out_specs=(pl.BlockSpec(memory_space=pl.ANY), vmem),
        scratch_shapes=[
            pltpu.VMEM((row_dev, n), BF16),
            pltpu.VMEM((n, col_dev), BF16),
            pltpu.VMEM((row_dev, col_dev), BF16),
            pltpu.SMEM((row_dev // BLOCK,), jnp.int32),
            pltpu.SemaphoreType.DMA((row_dev // BLOCK,)),
        ]
        + [pltpu.VMEM((n, row_dev), BF16)] * 3,
        compiler_params=pltpu.CompilerParams(vmem_limit_bytes=28 << 20),
        cost_estimate=pl.CostEstimate(flops=8 << 30, bytes_accessed=24 << 20, transcendentals=0),
    )(at, pattern, *rows, *first, *second, w, half, regrouped, pivot_loads, trailing)


def per_device(loads, nd_source, panel, trailing, pattern, owner):
    row_dev = panel.shape[0]
    row_count = lax.axis_size("row")
    slice_width = panel.shape[1]
    pivot_size = slice_width * lax.axis_size("col")
    share_size = row_dev // row_count
    row_place = lax.axis_index("row")
    root = owner[0]
    at = jnp.stack([row_place, lax.axis_index("col"), root])
    mine = panel.T
    both = lax.optimization_barrier

    moved = lax.ppermute(mine, ("row", "col"), transposed_place())
    packets = ring(pack(mine, loads, nd_source), X_SHIFT, "row")
    rows_other = lax.ppermute(mine, "col", Z_LO)
    (packet,) = small_call(choose_x, [(56, row_dev)], at, *packets)
    packet_other = lax.ppermute(packet, "row", Z_HI)
    (packet,) = small_call(choose_z, [(88, row_dev)], at, packet, packet_other)
    packet_other = lax.ppermute(packet, "row", CORE)
    pivot, digits = small_call(
        choose_core, [(slice_width, pivot_size), (8, pivot_size)], at, packet, packet_other
    )
    pivot, moved = both((pivot, moved))
    pivot_other = lax.ppermute(pivot, "col", Z_LO)
    moved_other = lax.ppermute(moved, "row", Z_HI)
    (pivot,) = small_call(pair_z_lo, [(2 * slice_width, pivot_size)], at, pivot, pivot_other)
    (rows,) = small_call(pair_z_lo, [(2 * slice_width, row_dev)], at, mine, rows_other)
    pivot = ring(pivot, Y_SHIFT, "col")
    (first,) = small_call(pair_z_hi, [(2 * slice_width, row_dev)], at, moved, moved_other)
    first = ring(first, X_SHIFT, "row")

    everyone = jnp.concatenate([packet[24:], packet_other[24:]], 0).reshape(row_count, 8, row_dev)
    regrouped = regroup(everyone, nd_source, row_place, row_place, share_size)
    pivot_source = digits[0].astype(jnp.int32) * BLOCK + digits[1].astype(jnp.int32)
    pivot_loads = regroup(everyone, pivot_source, row_place, root, share_size)

    pivot, rows, regrouped, pivot_loads = both((pivot, rows, regrouped, pivot_loads))
    rows = ring(rows, Y_SHIFT, "col")
    w_top, half_top, rest = upper_inverse(pivot, at)
    rest, first = both((rest, first))
    second = [lax.ppermute(piece, "row", CORE) for piece in first]
    w, half = lower_inverse(rest, w_top, half_top)
    trailing_out, loads_out = update(
        at, pattern, rows, first, second, w, half, regrouped, pivot_loads, trailing
    )
    return loads_out, trailing_out


def solution(mesh):
    return jax.shard_map(
        per_device,
        mesh=mesh,
        in_specs=(P(None, "row"), P("row"), P("row", "col"), P("row", "col"), P("row", "col"), P()),
        out_specs=(P(None, "row"), P("row", "col")),
        check_vma=False,
    )
```

```python
import jax
import jax.numpy as jnp
from jax import lax
from jax.experimental import pallas as pl
from jax.experimental.pallas import tpu as pltpu
from jax.sharding import PartitionSpec as P

HI = lax.Precision.HIGHEST
F32 = jnp.float32
BF16 = jnp.bfloat16
BLOCK = 128

X_SHIFT = {k: [(i, (i // 4 + k) % 4 * 4 + i % 4) for i in range(16)] for k in (1, 2, 3)}
Y_SHIFT = {k: [(i, (i // 2 + k) % 4 * 2 + i % 2) for i in range(8)] for k in (1, 2, 3)}
Z_HI = [(i, i ^ 2) for i in range(16)]
CORE = [(i, i ^ 1) for i in range(16)]
Z_LO = [(i, i ^ 1) for i in range(8)]


def transposed_place():
    pairs = []
    for row in range(16):
        for col in range(8):
            x, z_hi, core = row // 4, row // 2 % 2, row % 2
            y, z_lo = col // 2, col % 2
            pairs.append((row * 8 + col, ((y * 2 + z_lo) * 2 + core) * 8 + x * 2 + z_hi))
    return pairs


def ring(mine, shifts, axis):
    return [mine] + [lax.ppermute(mine, axis, shifts[k]) for k in (1, 2, 3)]


def pack_kernel(panel_ref, loads_ref, source_ref, out_ref):
    size = out_ref.shape[1] // 3
    source = jnp.concatenate([source_ref[k : k + 1, :] for k in range(size // BLOCK)], 1)
    digits = jnp.concatenate([source // BLOCK, source % BLOCK, jnp.zeros((6, size), jnp.int32)], 0)
    head = jnp.concatenate([panel_ref[:, :size].astype(F32), digits.astype(F32)], 0)
    head = jnp.concatenate([head[24 * c : 24 * c + 24] for c in range(3)], 1)
    loads = loads_ref[...]
    high = loads.astype(BF16).astype(F32)
    low = loads - high
    tail = jnp.concatenate([high, low, jnp.zeros((2, loads.shape[1]), F32)], 0)
    out_ref[...] = jnp.concatenate([head, tail], 0).astype(BF16)


def pack(mine, loads, source):
    return pl.pallas_call(
        pack_kernel,
        out_shape=jax.ShapeDtypeStruct((32, mine.shape[1]), BF16),
        compiler_params=pltpu.CompilerParams(vmem_limit_bytes=4 << 20),
    )(mine, loads, source.reshape(-1, BLOCK))


def small_call(kernel, shapes, scalars, *arrays):
    vmem = pl.BlockSpec(memory_space=pltpu.VMEM)
    return pl.pallas_call(
        kernel,
        out_shape=tuple(jax.ShapeDtypeStruct(shape, BF16) for shape in shapes),
        in_specs=[pl.BlockSpec(memory_space=pltpu.SMEM)] + [vmem] * len(arrays),
        out_specs=(vmem,) * len(shapes),
        compiler_params=pltpu.CompilerParams(vmem_limit_bytes=4 << 20),
    )(scalars, *arrays)


def choose_x(at_ref, p0, p1, p2, p3, out_ref):
    back = ((at_ref[0] >> 2) + 4 - (at_ref[2] >> 2)) & 3
    pieces = [p[...].astype(F32) for p in (p0, p1, p2, p3)]
    head = pieces[0][:24]
    for k in (1, 2, 3):
        head = jnp.where(back == k, pieces[k][:24], head)
    out_ref[...] = jnp.concatenate([head] + [p[24:] for p in pieces], 0).astype(BF16)


def choose_z(at_ref, p0, p1, out_ref):
    own, other = p0[...].astype(F32), p1[...].astype(F32)
    head = jnp.where(((at_ref[0] ^ at_ref[2]) & 2) == 0, own[:24], other[:24])
    out_ref[...] = jnp.concatenate([head, own[24:], other[24:]], 0).astype(BF16)


def choose_core(at_ref, p0, p1, pivot_ref, digits_ref):
    size = pivot_ref.shape[1]
    head = jnp.where(((at_ref[0] ^ at_ref[2]) & 1) == 0, p0[...].astype(F32)[:24], p1[...].astype(F32)[:24])
    head = jnp.concatenate([head[:, c * size : (c + 1) * size] for c in range(3)], 0)
    pivot_ref[...] = head[:64].astype(BF16)
    digits_ref[...] = head[64:].astype(BF16)


def pair_z_lo(at_ref, p0, p1, out_ref):
    own, other = p0[...], p1[...]
    low = (at_ref[1] & 1) == 0
    out_ref[...] = jnp.concatenate([jnp.where(low, own, other), jnp.where(low, other, own)], 0)


def pair_z_hi(at_ref, p0, p1, out_ref):
    own, other = p0[...], p1[...]
    low = (at_ref[0] & 2) == 0
    out_ref[...] = jnp.concatenate([jnp.where(low, own, other), jnp.where(low, other, own)], 0)


def regroup(window_of, source, row_place, target, share):
    arrived = lax.dynamic_slice_in_dim(window_of, target * share, share, 2)
    arrived = arrived.transpose(1, 0, 2).reshape(arrived.shape[1], -1)
    home = lax.div(source, share * 16)
    flip = home ^ row_place
    turn = ((row_place >> 2) + 4 - (home >> 2)) & 3
    place = (flip & 1) * 8 + (flip & 2) * 2 + turn
    slot = (place - home * 16) * share + source - target * share
    parts = jnp.take(arrived, slot, axis=1)
    return jnp.concatenate([parts[:3].astype(F32) + parts[3:6].astype(F32), jnp.zeros((5, slot.shape[0]), F32)], 0)


def block_inverse(rows):
    n = rows[0].shape[1]
    lane = lax.broadcasted_iota(jnp.int32, (8, n), 1)
    sub = lax.broadcasted_iota(jnp.int32, (8, n), 0)
    rows = list(rows)
    out = []
    for g in range(len(rows)):
        p = 8 * g
        below = range(g + 1, len(rows))
        strip = rows[g]
        cols = [jnp.broadcast_to(strip[:, p + k : p + k + 1], (8, n)) for k in range(8)]
        cols_below = {
            i: [jnp.broadcast_to(rows[i][:, p + k : p + k + 1], (8, n)) for k in range(8)] for i in below
        }
        in_block = (lane >= p) & (lane < p + 8)
        for i in below:
            rows[i] = jnp.where(in_block, 0.0, rows[i])
        pivots = None
        for k in range(8):
            d = jnp.broadcast_to(cols[k][k : k + 1, :], (8, n))
            r = 1.0 / d
            pivots = d if k == 0 else jnp.where(sub == k, d, pivots)
            m = jnp.where(sub > k, cols[k] * r, 0.0)
            piv = jnp.where(lane == p + k, 1.0, jnp.broadcast_to(strip[k : k + 1, :], (8, n)))
            strip = jnp.where((lane == p + k) & (sub > k), 0.0, strip) - m * piv
            piv = jnp.where((lane > p + k) & (lane < p + 8), 0.0, piv)
            u = [None] * 8
            for q in range(k + 1, 8):
                u[q] = jnp.broadcast_to(cols[q][k : k + 1, :], (8, n))
                cols[q] = cols[q] - m * u[q]
            for i in below:
                f = cols_below[i][k] * r
                for q in range(k + 1, 8):
                    cols_below[i][q] = cols_below[i][q] - f * u[q]
                rows[i] = rows[i] - f * piv
        s = lax.rsqrt(pivots)
        out.append(jnp.where(lane == sub + p, s, strip * s))
    return out


def eliminate(g_ref, w_ref, half_ref, blocks, first_row):
    n = g_ref.shape[0]
    B = BLOCK
    lane = lax.broadcasted_iota(jnp.int32, (B, n), 1)
    row = lax.broadcasted_iota(jnp.int32, (B, n), 0)
    lane_b = lax.broadcasted_iota(jnp.int32, (B, B), 1)
    row_b = lax.broadcasted_iota(jnp.int32, (B, B), 0)

    def step(k, carry):
        at = pl.multiple_of(k * B, B)
        diag = g_ref[pl.ds(at, B), pl.ds(at, B)]
        wk = jnp.concatenate(block_inverse([diag[8 * i : 8 * i + 8] for i in range(B // 8)]), 0)
        wk = jnp.where(lane_b <= row_b, wk, 0.0)
        here = (lane >= at) & (lane < at + B)
        strip = jnp.where(here, jnp.where(lane == row + at, 1.0, 0.0), g_ref[pl.ds(at, B), :])
        y = jnp.dot(wk, strip, precision=HI, preferred_element_type=F32)
        done = jnp.where(lane <= row + at, y, 0.0)
        to = pl.multiple_of(at - first_row, B)
        w_ref[pl.ds(to, B), :] = done
        half_ref[pl.ds(to, B), :] = done.astype(BF16)
        for j in range(blocks[0] + 1, n // B):

            @pl.when(j > k)
            def _():
                old = jnp.where(here, 0.0, g_ref[j * B : (j + 1) * B, :])
                g_ref[j * B : (j + 1) * B, :] = old - lax.dot_general(
                    y[:, j * B : (j + 1) * B],
                    y,
                    (((0,), (0,)), ((), ())),
                    precision=HI,
                    preferred_element_type=F32,
                )

        return carry

    lax.fori_loop(*blocks, step, 0)


def upper_kernel(at_ref, p0, p1, p2, p3, w_ref, half_ref, g_ref):
    for k, piece in enumerate((p0, p1, p2, p3)):
        at = pl.multiple_of((((at_ref[1] >> 1) + 4 - k) & 3) * BLOCK, BLOCK)
        g_ref[pl.ds(at, BLOCK), :] = piece[...].astype(F32)
    whole = g_ref[...]
    g_ref[...] = 0.5 * (whole + whole.T)
    eliminate(g_ref, w_ref, half_ref, (0, 2), 0)


def lower_kernel(in_ref, w_top, half_top, w_ref, half_ref, g_ref):
    top = in_ref.shape[0]
    g_ref[top:, :] = in_ref[...]
    w_ref[:top, :] = w_top[...]
    half_ref[:top, :] = half_top[...]
    eliminate(g_ref, w_ref, half_ref, (2, 4), 0)


def upper_inverse(pieces, at):
    n = pieces[0].shape[1]
    vmem = pl.BlockSpec(memory_space=pltpu.VMEM)

    def kernel(at_ref, p0, p1, p2, p3, w_ref, half_ref, rest_ref, g_ref):
        upper_kernel(at_ref, p0, p1, p2, p3, w_ref, half_ref, g_ref)
        rest_ref[...] = g_ref[n // 2 :, :]

    return pl.pallas_call(
        kernel,
        out_shape=(
            jax.ShapeDtypeStruct((n // 2, n), F32),
            jax.ShapeDtypeStruct((n // 2, n), BF16),
            jax.ShapeDtypeStruct((n // 2, n), F32),
        ),
        in_specs=[pl.BlockSpec(memory_space=pltpu.SMEM)] + [vmem] * 4,
        out_specs=(vmem,) * 3,
        scratch_shapes=[pltpu.VMEM((n, n), F32)],
        compiler_params=pltpu.CompilerParams(vmem_limit_bytes=8 << 20),
        cost_estimate=pl.CostEstimate(flops=10 << 30, bytes_accessed=4 * n * n, transcendentals=0),
    )(at, *pieces)


def lower_inverse(rest, w_top, half_top):
    n = rest.shape[1]
    vmem = pl.BlockSpec(memory_space=pltpu.VMEM)
    return pl.pallas_call(
        lower_kernel,
        out_shape=(jax.ShapeDtypeStruct((n, n), F32), jax.ShapeDtypeStruct((n, n), BF16)),
        in_specs=[vmem] * 3,
        out_specs=(vmem,) * 2,
        scratch_shapes=[pltpu.VMEM((n, n), F32)],
        compiler_params=pltpu.CompilerParams(vmem_limit_bytes=8 << 20),
        cost_estimate=pl.CostEstimate(flops=10 << 30, bytes_accessed=4 * n * n, transcendentals=0),
    )(rest, w_top, half_top)


def update_kernel(at_ref, pattern_ref, *refs):
    rows_in, first_in, second_in = refs[0:4], refs[4:8], refs[8:12]
    w_ref, half_ref, loads_ref, pivot_ref, trailing_ref, out_ref, loads_out_ref = refs[12:19]
    factor_ref, other_ref, new_ref, list_ref, sems = refs[19:24]
    raw_refs = refs[24:27]
    n = half_ref.shape[0]
    row_dev, col_dev = trailing_ref.shape
    x, y, core = at_ref[0] >> 2, at_ref[1] >> 1, at_ref[0] & 1

    def copy(source, s):
        at = pl.ds(pl.multiple_of(s * BLOCK, BLOCK), BLOCK)
        return pltpu.make_async_copy(source.at[at, :], out_ref.at[at, :], sems.at[s])

    def sort_strip(s, count):
        filled = pattern_ref[s, 0]
        for j in range(1, col_dev // BLOCK):
            filled = filled | pattern_ref[s, j]

        @pl.when(filled != 0)
        def _():
            list_ref[count] = s

        @pl.when(filled == 0)
        def _():
            copy(trailing_ref, s).start()

        return count + (filled != 0).astype(jnp.int32)

    count = lax.fori_loop(0, row_dev // BLOCK, sort_strip, 0)

    def assemble(raw_ref, pieces, spot):
        for k, piece in enumerate(pieces):
            at = pl.multiple_of(((spot + 4 - k) & 3) * BLOCK, BLOCK)
            raw_ref[pl.ds(at, BLOCK), :] = piece[...]

    assemble(raw_refs[0], rows_in, y)
    assemble(raw_refs[1], first_in, x)
    assemble(raw_refs[2], second_in, x)
    for c in range(0, row_dev, 512):
        part = lax.dot_general(
            raw_refs[0][:, c : c + 512], half_ref[...], (((0,), (1,)), ((), ())), preferred_element_type=F32
        )
        factor_ref[c : c + 512, :] = part.astype(BF16)
    for raw_ref, column in ((raw_refs[1], core * row_dev), (raw_refs[2], (1 - core) * row_dev)):
        for c in range(0, row_dev, 512):
            part = jnp.dot(half_ref[...], raw_ref[:, c : c + 512], preferred_element_type=F32).astype(BF16)
            other_ref[:, pl.ds(pl.multiple_of(column + c, 128), 512)] = part

    TILE = 512

    def strip_at(s):
        return pl.ds(pl.multiple_of(s * BLOCK, BLOCK), BLOCK)

    def pair_step(p, carry):
        last = 2 * p + 1 < count
        pair = (list_ref[2 * p], list_ref[jnp.where(last, 2 * p + 1, 2 * p)])
        left = jnp.concatenate([factor_ref[strip_at(s), :] for s in pair], 0)
        for t in range(0, col_dev, TILE):
            product = jnp.dot(left, other_ref[:, t : t + TILE], preferred_element_type=F32)
            for i, s in enumerate(pair):
                for j in range(0, TILE, BLOCK):
                    flag = pattern_ref[s, (t + j) // BLOCK].astype(F32)
                    old = trailing_ref[strip_at(s), t + j : t + j + BLOCK].astype(F32)
                    new = old - product[i * BLOCK : (i + 1) * BLOCK, j : j + BLOCK] * flag
                    new_ref[strip_at(s), t + j : t + j + BLOCK] = new.astype(BF16)
        copy(new_ref, pair[0]).start()

        @pl.when(last)
        def _():
            copy(new_ref, pair[1]).start()

        return carry

    lax.fori_loop(0, (count + 1) // 2, pair_step, 0)

    solve = lax.dot_general(
        pivot_ref[...], w_ref[...], (((1,), (1,)), ((), ())), precision=HI, preferred_element_type=F32
    )
    one = solve.astype(BF16)
    rest = solve - one.astype(F32)
    two = rest.astype(BF16)
    three = (rest - two.astype(F32)).astype(BF16)
    parts = jnp.concatenate([p.astype(F32) for p in (one, two, three)], 0).astype(BF16)
    change = lax.dot_general(parts, factor_ref[...], (((1,), (1,)), ((), ())), preferred_element_type=F32)
    loads_out_ref[...] = (loads_ref[...] - (change[:8] + change[8:16] + change[16:24]))[:3]

    @pl.when(at_ref[0] == at_ref[2])
    def _():
        loads_out_ref[:, :n] = solve[:3]

    lax.fori_loop(0, row_dev // BLOCK, lambda s, c: (copy(new_ref, s).wait(), c)[1], 0)


def update(at, pattern, rows, first, second, w, half, regrouped, pivot_loads, trailing):
    row_dev, col_dev = trailing.shape
    n = half.shape[0]
    smem = pl.BlockSpec(memory_space=pltpu.SMEM)
    vmem = pl.BlockSpec(memory_space=pltpu.VMEM)
    return pl.pallas_call(
        update_kernel,
        out_shape=(
            jax.ShapeDtypeStruct((row_dev, col_dev), BF16),
            jax.ShapeDtypeStruct((3, row_dev), F32),
        ),
        in_specs=[smem, smem] + [vmem] * 17,
        out_specs=(pl.BlockSpec(memory_space=pl.ANY), vmem),
        scratch_shapes=[
            pltpu.VMEM((row_dev, n), BF16),
            pltpu.VMEM((n, col_dev), BF16),
            pltpu.VMEM((row_dev, col_dev), BF16),
            pltpu.SMEM((row_dev // BLOCK,), jnp.int32),
            pltpu.SemaphoreType.DMA((row_dev // BLOCK,)),
        ]
        + [pltpu.VMEM((n, row_dev), BF16)] * 3,
        compiler_params=pltpu.CompilerParams(vmem_limit_bytes=28 << 20),
        cost_estimate=pl.CostEstimate(flops=8 << 30, bytes_accessed=24 << 20, transcendentals=0),
    )(at, pattern, *rows, *first, *second, w, half, regrouped, pivot_loads, trailing)


def per_device(loads, nd_source, panel, trailing, pattern, owner):
    row_dev = panel.shape[0]
    row_count = lax.axis_size("row")
    slice_width = panel.shape[1]
    pivot_size = slice_width * lax.axis_size("col")
    share_size = row_dev // row_count
    row_place = lax.axis_index("row")
    root = owner[0]
    at = jnp.stack([row_place, lax.axis_index("col"), root])
    mine = panel.T
    both = lax.optimization_barrier

    moved = lax.ppermute(mine, ("row", "col"), transposed_place())
    packets = ring(pack(mine, loads, nd_source), X_SHIFT, "row")
    rows_other = lax.ppermute(mine, "col", Z_LO)
    (packet,) = small_call(choose_x, [(56, row_dev)], at, *packets)
    packet_other = lax.ppermute(packet, "row", Z_HI)
    (packet,) = small_call(choose_z, [(88, row_dev)], at, packet, packet_other)
    packet_other = lax.ppermute(packet, "row", CORE)
    pivot, digits = small_call(
        choose_core, [(slice_width, pivot_size), (8, pivot_size)], at, packet, packet_other
    )
    pivot_other = lax.ppermute(pivot, "col", Z_LO)
    moved_other = lax.ppermute(moved, "row", Z_HI)
    (pivot,) = small_call(pair_z_lo, [(2 * slice_width, pivot_size)], at, pivot, pivot_other)
    (rows,) = small_call(pair_z_lo, [(2 * slice_width, row_dev)], at, mine, rows_other)
    pivot = ring(pivot, Y_SHIFT, "col")
    (first,) = small_call(pair_z_hi, [(2 * slice_width, row_dev)], at, moved, moved_other)
    first = ring(first, X_SHIFT, "row")

    everyone = jnp.concatenate([packet[24:], packet_other[24:]], 0).reshape(row_count, 8, row_dev)
    regrouped = regroup(everyone, nd_source, row_place, row_place, share_size)
    pivot_source = digits[0].astype(jnp.int32) * BLOCK + digits[1].astype(jnp.int32)
    pivot_loads = regroup(everyone, pivot_source, row_place, root, share_size)

    pivot, rows, regrouped, pivot_loads = both((pivot, rows, regrouped, pivot_loads))
    rows = ring(rows, Y_SHIFT, "col")
    w_top, half_top, rest = upper_inverse(pivot, at)
    rest, first = both((rest, first))
    second = [lax.ppermute(piece, "row", CORE) for piece in first]
    w, half = lower_inverse(rest, w_top, half_top)
    trailing_out, loads_out = update(
        at, pattern, rows, first, second, w, half, regrouped, pivot_loads, trailing
    )
    return loads_out, trailing_out


def solution(mesh):
    return jax.shard_map(
        per_device,
        mesh=mesh,
        in_specs=(P(None, "row"), P("row"), P("row", "col"), P("row", "col"), P("row", "col"), P()),
        out_specs=(P(None, "row"), P("row", "col")),
        check_vma=False,
    )
```
